32 devices in a mesh: prow: 8 (over z, x), pcol: 4 (over y, core).
Axes of the slice: x: 2, y: 2, z: 4, core: 2. Of those that a mesh axis runs over, the one named last changes fastest.
Arguments:
- rhs: float32 [31, 64, 2048], P(None, None, 'prow'), may hold values from -6 to 6
- factor: bfloat16 [98, 2048, 2048], P(None, 'prow', 'pcol'), may hold values from -0.03125 to 0.03125
- inverse: bfloat16 [31, 2048, 2048], P(None, 'pcol', 'prow')
- pattern: int32 [98], replicated, may hold values 0 or 1
Outputs:
- solution: float32 [31, 64, 2048], P(None, None, 'prow')
- forward_solution: float32 [31, 64, 2048], P(None, None, 'pcol')
The draws below stay inside these ranges and needn't reach their ends.
All inputs are finite; a program needn't handle non-finite values.
Results may differ from the reference program's by a relative error of at most 0.011.
Values sent between devices are 32-bit elements; how exact they have to be, the bound alone decides.
A program may use at most 128 MiB of HBM per device.

```python
import math
import jax
import jax.numpy as jnp
from jax import lax

W = 2048
R = 64
LEV = 5
NS = 31
NBLK = 98


def draw_inverse(key, part):
    first_key, second_key = jax.random.split(key)
    row_ids = lax.broadcasted_iota(jnp.int32, (NS, W, W), 1)
    col_ids = lax.broadcasted_iota(jnp.int32, (NS, W, W), 2)
    diagonal = jax.random.uniform(first_key, (NS, W, 1), jnp.float32, 1.0, 2.0)
    spread_part = jax.random.normal(second_key, (NS, W, W), jnp.float32) * 0.4 / math.sqrt(W)
    return jnp.where(row_ids == col_ids, diagonal, spread_part).astype(jnp.bfloat16)


def touch_ends(drawn, rng, low, largest):
    place = [jax.random.randint(jax.random.fold_in(rng, axis), (), 0, length) for axis, length in enumerate(drawn.shape)]
    widest = drawn.shape.index(max(drawn.shape))
    neighbour = place[:widest] + [(place[widest] + 1) % drawn.shape[widest]] + place[widest + 1:]
    return drawn.at[tuple(place)].set(low).at[tuple(neighbour)].set(largest)


def shard_levels(own_key, dims, cuts, low, largest):
    def one(axis_at, shards_of):
        heights = jax.random.uniform(jax.random.fold_in(jax.random.fold_in(own_key, 6), axis_at), (shards_of,), jnp.float32, low / len(cuts), largest / len(cuts))
        return jnp.repeat(jnp.exp(heights), dims[axis_at] // shards_of).reshape((-1,) + (1,) * (len(dims) - axis_at - 1))

    gain = one(*cuts[0])
    for cut in cuts[1:]:
        gain = gain * one(*cut)
    return gain


def scatter_about(own_key, dims, spread, reach, pieces=(), kind=jnp.bfloat16):
    gain = shard_levels(own_key, dims, pieces, -0.22, 0.18) if pieces else 1.0
    values = jax.random.normal(own_key, dims, jnp.float32) * spread * gain
    return jnp.minimum(jnp.maximum(values, -reach), reach).astype(kind)


def setup_inputs(seed: int = 0) -> dict:
    streams_of = jax.random.split(jax.random.key(seed), 5)
    return {
        "rhs": scatter_about(streams_of[0], (NS, R, W), 1.0, 6.0, ((2, 8),), jnp.float32),
        "factor": scatter_about(streams_of[1], (NBLK, W, W), (16 * W) ** -0.5, 0.03125, ((1, 8), (2, 4))),
        "inverse": draw_inverse(jax.random.fold_in(streams_of[4], 71), 0),
        "pattern": touch_ends((jax.random.randint(streams_of[3], (NBLK,), 0, 3) < 2).astype(jnp.int32), jax.random.fold_in(streams_of[3], 1), 0, 1),
    }


def block_start(tree_depth):
    return (tree_depth - 2) * 2 ** tree_depth + 2


def product(left, right, form):
    return jnp.einsum(form, left.astype(jnp.float32), right.astype(jnp.float32))


def reference(rhs, factor, inverse, pattern):
    live = pattern.astype(jnp.float32)
    partial_value = jnp.zeros(rhs.shape, jnp.float32)
    forward_levels = [None] * LEV
    for tree_depth in range(LEV - 1, -1, -1):
        first = 2 ** tree_depth - 1
        count = 2 ** tree_depth
        residual = rhs[first:first + count] - partial_value[first:first + count]
        rounded = lax.optimization_barrier(residual.astype(jnp.bfloat16))
        forward = product(rounded, inverse[first:first + count], "nrc,nwc->nrw")
        forward_levels[tree_depth] = forward
        narrow = lax.optimization_barrier(forward.astype(jnp.bfloat16))
        if tree_depth > 0:
            start = block_start(tree_depth)
            weights = live[start:start + count * tree_depth].reshape(count, tree_depth)
            for upward in range(1, tree_depth + 1):
                blocks = factor[start + upward - 1:start + count * tree_depth:tree_depth]
                terms = product(narrow, blocks, "nrc,nwc->nrw") * weights[:, upward - 1][:, None, None]
                groups = count >> upward
                terms = terms.reshape((groups, 2 ** upward) + terms.shape[1:]).sum(axis=1)
                target = 2 ** (tree_depth - upward) - 1
                partial_value = partial_value.at[target:target + groups].add(terms)
    solved = [None] * LEV
    solved_narrow = [None] * LEV
    for tree_depth in range(LEV):
        first = 2 ** tree_depth - 1
        count = 2 ** tree_depth
        target_vec = forward_levels[tree_depth]
        if tree_depth > 0:
            start = block_start(tree_depth)
            weights = live[start:start + count * tree_depth].reshape(count, tree_depth)
            gathered = jnp.zeros(target_vec.shape, jnp.float32)
            for upward in range(1, tree_depth + 1):
                blocks = factor[start + upward - 1:start + count * tree_depth:tree_depth]
                above = jnp.repeat(solved_narrow[tree_depth - upward], 2 ** upward, axis=0)
                gathered = gathered + product(above, blocks, "nrw,nwc->nrc") * weights[:, upward - 1][:, None, None]
            target_vec = target_vec - gathered
        rounded = lax.optimization_barrier(target_vec.astype(jnp.bfloat16))
        solution = product(rounded, inverse[first:first + count], "nrw,nwc->nrc")
        solved[tree_depth] = solution
        solved_narrow[tree_depth] = lax.optimization_barrier(solution.astype(jnp.bfloat16))
    return (jnp.concatenate(solved, axis=0), jnp.concatenate(forward_levels, axis=0))
```

```python
import jax
import jax.numpy as jnp
from jax import lax
from jax.experimental import pallas as pl
from jax.experimental.pallas import tpu as pltpu
from jax.sharding import PartitionSpec as P

LEV = 5
CHUNKS = {4: 4, 3: 2, 2: 1, 1: 1, 0: 1}
MESH = pl.DeviceIdType.MESH


def block_start(tree_depth):
    return (tree_depth - 2) * 2**tree_depth + 2


def split_rows(prow):
    minor = 1
    while minor * minor * 4 <= prow:
        minor *= 2
    return prow // minor, minor


def tasks_of(order):
    tasks = []
    for depth in order:
        size = 2**depth // CHUNKS[depth]
        for c in range(CHUNKS[depth]):
            tasks.append((depth, 2**depth - 1 + c * size, size))
    return tasks


def run_tasks(tasks, make, needs):
    done = set()
    live = {}
    waiting = list(tasks)
    while waiting or live:
        for task in list(waiting):
            if all(other in done for other in tasks if needs(task, other)):
                live[task] = make(*task)
                waiting.remove(task)
        for task in list(live):
            try:
                next(live[task])
            except StopIteration:
                done.add(task)
                del live[task]


def overlaps(low_task, high_task):
    depth, first, size = low_task
    up_depth, up_first, up_size = high_task
    if up_depth != depth - 1:
        return False
    parents = {(n + 1) // 2 - 1 for n in range(first, first + size)}
    return any(up_first <= p < up_first + up_size for p in parents)


def make_kernel(A, B, Y, NS, R, WC, WR):
    r = R // (A * B)
    half = R // 2
    inner = 2 ** (LEV - 1) - 1

    def kernel(
        rhs_h, fac_h, inv_h, pat, sol_h, fwd_h,
        rhs, fac, inv, src, recv1, recv2, yout, tout, csrc, cr_f, cr_b, yr_f, yr_b, res, sol,
        lsem, ssem, rsem,
    ):
        prow = lax.axis_index("prow")
        pcol = lax.axis_index("pcol")
        my_a, my_b = prow // B, prow % B
        my_y, my_c = pcol // 2, pcol % 2
        other_c = 1 - my_c
        counter = [0]
        lcounter = [0]

        loads = {}

        def load(key, source, target):
            copy = pltpu.make_async_copy(source, target, lsem.at[lcounter[0]])
            lcounter[0] += 1
            copy.start()
            loads[key] = copy

        def need(key):
            if key in loads:
                loads.pop(key).wait()

        for depth in range(LEV - 1, -1, -1):
            count = 2**depth
            nodes = pl.ds(count - 1, count)
            load(("rhs", depth), rhs_h.at[nodes], rhs.at[nodes])
            load(("inv", depth), inv_h.at[nodes], inv.at[nodes])
            if depth:
                blocks = pl.ds(block_start(depth), count * depth)
                load(("fac", depth), fac_h.at[blocks], fac.at[blocks])

        barrier = pltpu.get_barrier_semaphore()
        peers = [{"prow": my_a * B + (my_b + o) % B} for o in range(1, B)]
        peers += [{"prow": ((my_a + o) % A) * B + my_b} for o in range(1, A)]
        peers += [{"pcol": my_y * 2 + other_c}]
        peers += [{"pcol": ((my_y + o) % Y) * 2 + my_c} for o in range(1, Y)]
        for peer in peers:
            pl.semaphore_signal(barrier, inc=1, device_id=peer, device_id_type=MESH)
        csrc[...] = jnp.zeros(csrc.shape, jnp.float32)
        pl.semaphore_wait(barrier, len(peers))

        def send(source, target, peer):
            k = counter[0]
            counter[0] += 1
            copy = pltpu.make_async_remote_copy(
                src_ref=source, dst_ref=target, send_sem=ssem.at[k], recv_sem=rsem.at[k],
                device_id=peer, device_id_type=MESH,
            )
            copy.start()
            return copy

        def wait_all(copies):
            for copy in copies:
                copy.wait()

        def put_parts(value, n):
            for q in range(A * B):
                src[q // A, q % A, n] = value[q * r : (q + 1) * r]

        def get_parts(ref, n):
            return jnp.concatenate(
                [ref[q // A, q % A, n] for q in range(A * B)], axis=0
            )

        def get_halves(ref, n):
            return jnp.concatenate([ref[0, n], ref[1, n]], axis=0)

        def reduce_rows(first, size, out, finish):
            nodes = pl.ds(first, size)
            copies = []
            for o in range(1, B):
                b = (my_b + o) % B
                copies.append(
                    send(src.at[b, :, nodes], recv1.at[o - 1, :, nodes], {"prow": my_a * B + b})
                )
            yield
            wait_all(copies)
            for o in range(1, B):
                src[my_b, :, nodes] += recv1[o - 1, :, nodes]
            copies = []
            for o in range(1, A):
                a = (my_a + o) % A
                copies.append(
                    send(src.at[my_b, a, nodes], recv2.at[o - 1, nodes], {"prow": a * B + my_b})
                )
            yield
            wait_all(copies)
            total = src[my_b, my_a, nodes]
            for o in range(1, A):
                total = total + recv2[o - 1, nodes]
            out[my_b, my_a, nodes] = finish(total, nodes)
            copies = []
            for o in range(1, A):
                a = (my_a + o) % A
                part = out.at[my_b, my_a, nodes]
                copies.append(send(part, part, {"prow": a * B + my_b}))
            yield
            wait_all(copies)
            copies = []
            for o in range(1, B):
                b = (my_b + o) % B
                part = out.at[my_b, :, nodes]
                copies.append(send(part, part, {"prow": my_a * B + b}))
            yield
            wait_all(copies)

        def reduce_columns(first, size, cr, yr, out, finish):
            nodes = pl.ds(first, size)
            core = {"pcol": my_y * 2 + other_c}
            copies = [send(csrc.at[other_c, nodes], cr.at[nodes], core)]
            yield
            wait_all(copies)
            yr[my_y, nodes] = csrc[my_c, nodes] + cr[nodes]
            copies = []
            for o in range(1, Y):
                part = yr.at[my_y, nodes]
                copies.append(send(part, part, {"pcol": ((my_y + o) % Y) * 2 + my_c}))
            yield
            wait_all(copies)
            total = yr[0, nodes]
            for y in range(1, Y):
                total = total + yr[y, nodes]
            out[my_c, nodes] = finish(total, nodes)
            part = out.at[my_c, nodes]
            copies = [send(part, part, core)]
            yield
            wait_all(copies)

        def forward_task(depth, first, size):
            need(("rhs", depth))
            if depth < LEV - 1:
                mine = pl.ds(pl.multiple_of(my_c * half, half), half)
                yield from reduce_columns(
                    first, size, cr_f, yr_f, res,
                    lambda total, nodes: rhs[nodes, mine] - total,
                )
            need(("inv", depth))

            def solve(n, _):
                value = rhs[n] if depth == LEV - 1 else get_halves(res, n)
                put_parts(
                    lax.dot_general(
                        value.astype(jnp.bfloat16), inv[n], (((1,), (1,)), ((), ())),
                        preferred_element_type=jnp.float32,
                    ),
                    n,
                )
                return _

            lax.fori_loop(first, first + size, solve, 0)
            yield from reduce_rows(first, size, yout, lambda total, nodes: total)
            if depth:
                need(("fac", depth))
                start = block_start(depth)

                def push(m, _):
                    narrow = get_parts(yout, m)
                    base = start + (m - (2**depth - 1)) * depth
                    for up in range(1, depth + 1):
                        weight = pat[base + up - 1].astype(jnp.float32)
                        terms = lax.dot_general(
                            narrow.astype(jnp.bfloat16), fac[base + up - 1],
                            (((1,), (1,)), ((), ())), preferred_element_type=jnp.float32,
                        ) * weight
                        above = (m + 1) // 2**up - 1
                        csrc[0, above] += terms[:half]
                        csrc[1, above] += terms[half:]
                    return _

                lax.fori_loop(first, first + size, push, 0)

        def backward_task(depth, first, size):
            if depth:
                start = block_start(depth)

                def pull(n, _):
                    base = start + (n - (2**depth - 1)) * depth
                    total = jnp.zeros((R, WC), jnp.float32)
                    for up in range(1, depth + 1):
                        above = (n + 1) // 2**up - 1
                        weight = pat[base + up - 1].astype(jnp.float32)
                        total = total + weight * jnp.dot(
                            get_halves(sol, above).astype(jnp.bfloat16), fac[base + up - 1],
                            preferred_element_type=jnp.float32,
                        )
                    put_parts(total, n)
                    return _

                lax.fori_loop(first, first + size, pull, 0)
                yield from reduce_rows(
                    first, size, tout,
                    lambda total, nodes: yout[my_b, my_a, nodes] - total,
                )
            target = tout if depth else yout

            def solve(n, _):
                value = jnp.dot(
                    get_parts(target, n).astype(jnp.bfloat16), inv[n],
                    preferred_element_type=jnp.float32,
                )
                csrc[0, n] = value[:half]
                csrc[1, n] = value[half:]
                return _

            lax.fori_loop(first, first + size, solve, 0)
            yield from reduce_columns(
                first, size, cr_b, yr_b, sol, lambda total, nodes: total
            )

        run_tasks(
            tasks_of(range(LEV - 1, -1, -1)), forward_task, lambda task, other: overlaps(other, task)
        )
        out_copy = pltpu.make_async_copy(yout, fwd_h, lsem.at[lcounter[0]])
        out_copy.start()
        run_tasks(tasks_of(range(LEV)), backward_task, lambda task, other: overlaps(task, other))
        sol_copy = pltpu.make_async_copy(sol, sol_h, lsem.at[lcounter[0] + 1])
        sol_copy.start()
        out_copy.wait()
        sol_copy.wait()

    f32, bf16 = jnp.float32, jnp.bfloat16
    ntask = sum(CHUNKS.values())
    row_sends = 2 * (A - 1 + B - 1)
    col_sends = 1 + Y
    sends = ntask * (row_sends + col_sends) * 2
    blocks = block_start(LEV)
    scratch = [
        pltpu.VMEM((NS, R, WR), f32),
        pltpu.VMEM((blocks, WR, WC), bf16),
        pltpu.VMEM((NS, WC, WR), bf16),
        pltpu.VMEM((B, A, NS, r, WC), f32),
        pltpu.VMEM((B - 1, A, NS, r, WC), f32),
        pltpu.VMEM((A - 1, NS, r, WC), f32),
        pltpu.VMEM((B, A, NS, r, WC), f32),
        pltpu.VMEM((B, A, NS, r, WC), f32),
        pltpu.VMEM((2, NS, half, WR), f32),
        pltpu.VMEM((inner, half, WR), f32),
        pltpu.VMEM((NS, half, WR), f32),
        pltpu.VMEM((Y, inner, half, WR), f32),
        pltpu.VMEM((Y, NS, half, WR), f32),
        pltpu.VMEM((2, inner, half, WR), f32),
        pltpu.VMEM((2, NS, half, WR), f32),
        pltpu.SemaphoreType.DMA((3 * LEV + 2,)),
        pltpu.SemaphoreType.DMA((sends,)),
        pltpu.SemaphoreType.DMA((sends,)),
    ]
    any_spec = pl.BlockSpec(memory_space=pl.ANY)
    return pl.pallas_call(
        kernel,
        out_shape=(
            jax.ShapeDtypeStruct((2, NS, half, WR), f32),
            jax.ShapeDtypeStruct((B, A, NS, r, WC), f32),
        ),
        in_specs=[any_spec, any_spec, any_spec, pl.BlockSpec(memory_space=pltpu.SMEM)],
        out_specs=(any_spec, any_spec),
        scratch_shapes=scratch,
        cost_estimate=pl.CostEstimate(
            flops=4 * R * WR * WC * (blocks + NS),
            bytes_accessed=2 * WR * WC * (blocks + NS) + 8 * NS * R * (WC + WR),
            transcendentals=0,
        ),
        compiler_params=pltpu.CompilerParams(
            collective_id=0, has_side_effects=True, vmem_limit_bytes=64 * 1024 * 1024 - 65536
        ),
    )


def solution(mesh):
    A, B = split_rows(mesh.shape["prow"])
    Y = mesh.shape["pcol"] // 2

    def per_device(rhs, factor, inverse, pattern):
        NS, R, WR = rhs.shape
        WC = inverse.shape[1]
        sol, fwd = make_kernel(A, B, Y, NS, R, WC, WR)(rhs, factor, inverse, pattern)
        sol = jnp.transpose(sol, (1, 0, 2, 3)).reshape(NS, R, WR)
        fwd = jnp.transpose(fwd, (2, 0, 1, 3, 4)).reshape(NS, R, WC)
        return sol, fwd

    in_specs = (P(None, None, "prow"), P(None, "prow", "pcol"), P(None, "pcol", "prow"), P())
    out_specs = (P(None, None, "prow"), P(None, None, "pcol"))
    return jax.shard_map(
        per_device, mesh=mesh, in_specs=in_specs, out_specs=out_specs, check_vma=False
    )
```

```python
import functools

import jax
import jax.numpy as jnp
from jax import lax
from jax.experimental import pallas as pl
from jax.experimental.pallas import tpu as pltpu
from jax.sharding import PartitionSpec as P

LEV = 5
CHUNKS = {4: 8, 3: 4, 2: 2, 1: 1, 0: 1}
DIRECT = 2
MESH = pl.DeviceIdType.MESH


def block_start(tree_depth):
    return (tree_depth - 2) * 2**tree_depth + 2


def split_rows(prow):
    minor = 1
    while minor * minor * 4 <= prow:
        minor *= 2
    return prow // minor, minor


def tasks_of(order):
    tasks = []
    for depth in order:
        size = 2**depth // CHUNKS[depth]
        for c in range(CHUNKS[depth]):
            tasks.append((depth, 2**depth - 1 + c * size, size))
    return tasks


def run_tasks(tasks, make, needs, fillers, filler_needs, blocks):
    done = set()
    live = {}
    heavy = []
    waiting = list(tasks)
    left = list(fillers)

    def advance(task):
        try:
            if next(live[task]) == "matmul":
                heavy.append(task)
        except StopIteration:
            done.add(task)
            del live[task]

    while waiting or live or left:
        started = set()
        for task in list(waiting):
            ready = all(other in done for other in tasks if needs(task, other))
            ready = ready and not any(blocks(filler, task) for filler in left)
            if ready and task[0] not in started:
                started.add(task[0])
                live[task] = make(*task)
                waiting.remove(task)
        for task in list(live):
            if task not in heavy:
                advance(task)
        for task in list(heavy):
            heavy.remove(task)
            advance(task)
        for filler in list(left):
            if all(other in done for other in tasks if filler_needs(filler, other)):
                left.remove(filler)
                fillers[filler]()
                break


def overlaps(low_task, high_task):
    depth, first, size = low_task
    up_depth, up_first, up_size = high_task
    if up_depth != depth - 1:
        return False
    parents = {(n + 1) // 2 - 1 for n in range(first, first + size)}
    return any(up_first <= p < up_first + up_size for p in parents)


def far_above(low_task, high_task):
    depth, first, size = low_task
    up_depth, up_first, up_size = high_task
    if up_depth > depth - 2:
        return False
    above = {(n + 1) // 2 ** (depth - up_depth) - 1 for n in range(first, first + size)}
    return any(up_first <= p < up_first + up_size for p in above)


def make_kernel(A, B, Y, NS, R, WC, WR):
    r = R // (A * B)
    half = R // 2
    inner = 2 ** (LEV - 1) - 1

    def kernel(
        rhs_h, fac_h, inv_h, pat, sol_h, fwd_h,
        rhs, fac, inv, src, recv1, recv2, recv3, yout, tout, csrc, cr_f, cr_b, yr_f, yr_b, res, sol,
        lsem, ssem, rsem,
    ):
        prow = lax.axis_index("prow")
        pcol = lax.axis_index("pcol")
        my_a, my_b = prow // B, prow % B
        my_y, my_c = pcol // 2, pcol % 2
        other_c = 1 - my_c
        counter = [0]
        lcounter = [0]

        loads = {}

        def load(key, source, target):
            copy = pltpu.make_async_copy(source, target, lsem.at[lcounter[0]])
            lcounter[0] += 1
            copy.start()
            loads[key] = copy

        def need(key):
            if key in loads:
                loads.pop(key).wait()

        for depth in range(LEV - 1, -1, -1):
            count = 2**depth
            nodes = pl.ds(count - 1, count)
            load(("rhs", depth), rhs_h.at[nodes], rhs.at[nodes])
            load(("inv", depth), inv_h.at[nodes], inv.at[nodes])
            if depth:
                blocks = pl.ds(block_start(depth), count * depth)
                load(("fac", depth), fac_h.at[blocks], fac.at[blocks])

        barrier = pltpu.get_barrier_semaphore()
        peers = [{"prow": (prow + o) % (A * B)} for o in range(1, A * B)]
        peers += [{"pcol": my_y * 2 + other_c}]
        peers += [{"pcol": ((my_y + o) % Y) * 2 + my_c} for o in range(1, Y)]
        for peer in peers:
            pl.semaphore_signal(barrier, inc=1, device_id=peer, device_id_type=MESH)
        csrc[...] = jnp.zeros(csrc.shape, jnp.float32)
        pl.semaphore_wait(barrier, len(peers))

        def send(source, target, peer):
            k = counter[0]
            counter[0] += 1
            copy = pltpu.make_async_remote_copy(
                src_ref=source, dst_ref=target, send_sem=ssem.at[k], recv_sem=rsem.at[k],
                device_id=peer, device_id_type=MESH,
            )
            copy.start()
            return copy

        def wait_all(copies):
            for copy in copies:
                copy.wait()

        def put_parts(value, n):
            for q in range(A * B):
                src[q % B, q // B, n] = value[q * r : (q + 1) * r]

        def get_parts(ref, n):
            return jnp.concatenate(
                [ref[q % B, q // B, n] for q in range(A * B)], axis=0
            )

        def get_halves(ref, n):
            return jnp.concatenate([ref[0, n], ref[1, n]], axis=0)

        def reduce_rows_direct(first, size, out, finish):
            nodes = pl.ds(first, size)
            others = [(prow + o) % (A * B) for o in range(1, A * B)]
            copies = []
            for k, q in enumerate(others):
                copies.append(
                    send(src.at[q % B, q // B, nodes], recv3.at[k, nodes], {"prow": q})
                )
            yield
            wait_all(copies)
            total = src[my_b, my_a, nodes]
            for k in range(A * B - 1):
                total = total + recv3[k, nodes]
            out[my_b, my_a, nodes] = finish(total, nodes)
            part = out.at[my_b, my_a, nodes]
            copies = [send(part, part, {"prow": q}) for q in others]
            yield
            wait_all(copies)

        def reduce_rows(depth, first, size, out, finish):
            if depth <= DIRECT:
                yield from reduce_rows_direct(first, size, out, finish)
                return
            nodes = pl.ds(first, size)
            copies = []
            for o in range(1, B):
                b = (my_b + o) % B
                copies.append(
                    send(src.at[b, :, nodes], recv1.at[o - 1, :, nodes], {"prow": my_a * B + b})
                )
            yield
            wait_all(copies)
            for o in range(1, B):
                src[my_b, :, nodes] += recv1[o - 1, :, nodes]
            copies = []
            for o in range(1, A):
                a = (my_a + o) % A
                copies.append(
                    send(src.at[my_b, a, nodes], recv2.at[o - 1, nodes], {"prow": a * B + my_b})
                )
            yield
            wait_all(copies)
            total = src[my_b, my_a, nodes]
            for o in range(1, A):
                total = total + recv2[o - 1, nodes]
            out[my_b, my_a, nodes] = finish(total, nodes)
            copies = []
            for o in range(1, A):
                a = (my_a + o) % A
                part = out.at[my_b, my_a, nodes]
                copies.append(send(part, part, {"prow": a * B + my_b}))
            yield
            wait_all(copies)
            copies = []
            for o in range(1, B):
                b = (my_b + o) % B
                part = out.at[my_b, :, nodes]
                copies.append(send(part, part, {"prow": my_a * B + b}))
            yield
            wait_all(copies)

        def reduce_columns(depth, first, size, cr, yr, out, finish):
            nodes = pl.ds(first, size)
            core = {"pcol": my_y * 2 + other_c}
            copies = [send(csrc.at[other_c, nodes], cr.at[nodes], core)]
            yield
            wait_all(copies)
            yr[my_y, nodes] = csrc[my_c, nodes] + cr[nodes]
            copies = []
            for o in range(1, Y):
                part = yr.at[my_y, nodes]
                copies.append(send(part, part, {"pcol": ((my_y + o) % Y) * 2 + my_c}))
            yield
            wait_all(copies)
            total = yr[0, nodes]
            for y in range(1, Y):
                total = total + yr[y, nodes]
            out[my_c, nodes] = finish(total, nodes)
            part = out.at[my_c, nodes]
            copies = [send(part, part, core)]
            yield
            wait_all(copies)

        def forward_task(depth, first, size):
            need(("rhs", depth))
            if depth < LEV - 1:
                mine = pl.ds(pl.multiple_of(my_c * half, half), half)
                yield from reduce_columns(
                    depth, first, size, cr_f, yr_f, res,
                    lambda total, nodes: rhs[nodes, mine] - total,
                )
                yield "matmul"
            need(("inv", depth))

            def solve(n, _):
                value = rhs[n] if depth == LEV - 1 else get_halves(res, n)
                put_parts(
                    lax.dot_general(
                        value.astype(jnp.bfloat16), inv[n], (((1,), (1,)), ((), ())),
                        preferred_element_type=jnp.float32,
                    ),
                    n,
                )
                return _

            lax.fori_loop(first, first + size, solve, 0)
            yield from reduce_rows(depth, first, size, yout, lambda total, nodes: total)
            if depth:
                yield "matmul"
                push_up(depth, first, size, [1])

        def push_up(depth, first, size, ups):
            need(("fac", depth))
            start = block_start(depth)

            def push(m, _):
                narrow = get_parts(yout, m)
                base = start + (m - (2**depth - 1)) * depth
                for up in ups:
                    weight = pat[base + up - 1].astype(jnp.float32)
                    terms = lax.dot_general(
                        narrow.astype(jnp.bfloat16), fac[base + up - 1],
                        (((1,), (1,)), ((), ())), preferred_element_type=jnp.float32,
                    ) * weight
                    above = (m + 1) // 2**up - 1
                    csrc[0, above] += terms[:half]
                    csrc[1, above] += terms[half:]
                return _

            lax.fori_loop(first, first + size, push, 0)

        def pull_down(depth, first, size, ups, add):
            start = block_start(depth)

            def pull(n, _):
                base = start + (n - (2**depth - 1)) * depth
                total = get_parts(src, n) if add else jnp.zeros((R, WC), jnp.float32)
                for up in ups:
                    above = (n + 1) // 2**up - 1
                    weight = pat[base + up - 1].astype(jnp.float32)
                    total = total + weight * jnp.dot(
                        get_halves(sol, above).astype(jnp.bfloat16), fac[base + up - 1],
                        preferred_element_type=jnp.float32,
                    )
                put_parts(total, n)
                return _

            lax.fori_loop(first, first + size, pull, 0)

        def backward_task(depth, first, size):
            if depth:
                pull_down(depth, first, size, [1], depth > 1)
                yield from reduce_rows(
                    depth, first, size, tout,
                    lambda total, nodes: yout[my_b, my_a, nodes] - total,
                )
                yield "matmul"
            target = tout if depth else yout

            def solve(n, _):
                value = jnp.dot(
                    get_parts(target, n).astype(jnp.bfloat16), inv[n],
                    preferred_element_type=jnp.float32,
                )
                csrc[0, n] = value[:half]
                csrc[1, n] = value[half:]
                return _

            lax.fori_loop(first, first + size, solve, 0)
            yield from reduce_columns(
                depth, first, size, cr_b, yr_b, sol, lambda total, nodes: total
            )

        up_tasks = tasks_of(range(LEV - 1, -1, -1))
        late = {
            t: functools.partial(push_up, *t, range(2, t[0] + 1)) for t in up_tasks if t[0] > 1
        }
        run_tasks(
            up_tasks, forward_task, lambda task, other: overlaps(other, task),
            late, lambda filler, other: other == filler, far_above,
        )
        out_copy = pltpu.make_async_copy(yout, fwd_h, lsem.at[lcounter[0]])
        out_copy.start()
        down_tasks = tasks_of(range(LEV))
        early = {
            t: functools.partial(pull_down, *t, range(2, t[0] + 1), False)
            for t in down_tasks if t[0] > 1
        }
        run_tasks(
            down_tasks, backward_task, overlaps,
            early, far_above, lambda filler, task: filler == task,
        )
        sol_copy = pltpu.make_async_copy(sol, sol_h, lsem.at[lcounter[0] + 1])
        sol_copy.start()
        out_copy.wait()
        sol_copy.wait()

    f32, bf16 = jnp.float32, jnp.bfloat16
    sends = 0
    for depth in range(LEV):
        rows = A * B - 1 if depth <= DIRECT else A + B - 2
        sends += CHUNKS[depth] * 2 * (2 * rows + 1 + Y)
    blocks = block_start(LEV)
    scratch = [
        pltpu.VMEM((NS, R, WR), f32),
        pltpu.VMEM((blocks, WR, WC), bf16),
        pltpu.VMEM((NS, WC, WR), bf16),
        pltpu.VMEM((B, A, NS, r, WC), f32),
        pltpu.VMEM((B - 1, A, NS, r, WC), f32),
        pltpu.VMEM((A - 1, NS, r, WC), f32),
        pltpu.VMEM((A * B - 1, 2 ** (DIRECT + 1) - 1, r, WC), f32),
        pltpu.VMEM((B, A, NS, r, WC), f32),
        pltpu.VMEM((B, A, NS, r, WC), f32),
        pltpu.VMEM((2, NS, half, WR), f32),
        pltpu.VMEM((inner, half, WR), f32),
        pltpu.VMEM((NS, half, WR), f32),
        pltpu.VMEM((Y, inner, half, WR), f32),
        pltpu.VMEM((Y, NS, half, WR), f32),
        pltpu.VMEM((2, inner, half, WR), f32),
        pltpu.VMEM((2, NS, half, WR), f32),
        pltpu.SemaphoreType.DMA((3 * LEV + 2,)),
        pltpu.SemaphoreType.DMA((sends,)),
        pltpu.SemaphoreType.DMA((sends,)),
    ]
    any_spec = pl.BlockSpec(memory_space=pl.ANY)
    return pl.pallas_call(
        kernel,
        out_shape=(
            jax.ShapeDtypeStruct((2, NS, half, WR), f32),
            jax.ShapeDtypeStruct((B, A, NS, r, WC), f32),
        ),
        in_specs=[any_spec, any_spec, any_spec, pl.BlockSpec(memory_space=pltpu.SMEM)],
        out_specs=(any_spec, any_spec),
        scratch_shapes=scratch,
        cost_estimate=pl.CostEstimate(
            flops=4 * R * WR * WC * (blocks + NS),
            bytes_accessed=2 * WR * WC * (blocks + NS) + 8 * NS * R * (WC + WR),
            transcendentals=0,
        ),
        compiler_params=pltpu.CompilerParams(
            collective_id=0, has_side_effects=True, vmem_limit_bytes=64 * 1024 * 1024 - 65536
        ),
    )


def solution(mesh):
    A, B = split_rows(mesh.shape["prow"])
    Y = mesh.shape["pcol"] // 2

    def per_device(rhs, factor, inverse, pattern):
        NS, R, WR = rhs.shape
        WC = inverse.shape[1]
        sol, fwd = make_kernel(A, B, Y, NS, R, WC, WR)(rhs, factor, inverse, pattern)
        sol = jnp.transpose(sol, (1, 0, 2, 3)).reshape(NS, R, WR)
        fwd = jnp.transpose(fwd, (2, 1, 0, 3, 4)).reshape(NS, R, WC)
        return sol, fwd

    in_specs = (P(None, None, "prow"), P(None, "prow", "pcol"), P(None, "pcol", "prow"), P())
    out_specs = (P(None, None, "prow"), P(None, None, "pcol"))
    return jax.shard_map(
        per_device, mesh=mesh, in_specs=in_specs, out_specs=out_specs, check_vma=False
    )
```

```python
import functools

import jax
import jax.numpy as jnp
from jax import lax
from jax.experimental import pallas as pl
from jax.experimental.pallas import tpu as pltpu
from jax.sharding import PartitionSpec as P

LEV = 5
CHUNKS = {4: 8, 3: 8, 2: 4, 1: 2, 0: 1}
DIRECT = 2
MESH = pl.DeviceIdType.MESH


def block_start(tree_depth):
    return (tree_depth - 2) * 2**tree_depth + 2


def split_rows(prow):
    minor = 1
    while minor * minor * 4 <= prow:
        minor *= 2
    return prow // minor, minor


def tasks_of(order):
    tasks = []
    for depth in order:
        size = 2**depth // CHUNKS[depth]
        for c in range(CHUNKS[depth]):
            tasks.append((depth, 2**depth - 1 + c * size, size))
    return tasks


def run_tasks(tasks, make, needs, fillers, filler_needs, blocks):
    done = set()
    live = {}
    heavy = []
    waiting = list(tasks)
    left = list(fillers)

    def advance(task):
        try:
            if next(live[task]) == "matmul":
                heavy.append(task)
        except StopIteration:
            done.add(task)
            del live[task]

    while waiting or live or left:
        started = set()
        for task in list(waiting):
            ready = all(other in done for other in tasks if needs(task, other))
            ready = ready and not any(blocks(filler, task) for filler in left)
            if ready and task[0] not in started:
                started.add(task[0])
                live[task] = make(*task)
                waiting.remove(task)
        for task in list(live):
            if task not in heavy:
                advance(task)
        for task in list(heavy):
            heavy.remove(task)
            advance(task)
        for filler in list(left):
            if all(other in done for other in tasks if filler_needs(filler, other)):
                left.remove(filler)
                fillers[filler]()
                break


def overlaps(low_task, high_task):
    depth, first, size = low_task
    up_depth, up_first, up_size = high_task
    if up_depth != depth - 1:
        return False
    parents = {(n + 1) // 2 - 1 for n in range(first, first + size)}
    return any(up_first <= p < up_first + up_size for p in parents)


def few_in_flight(depth, first, forward):
    if depth == DIRECT + 1:
        place = first - (2**depth - 1)
        return place >= 2**depth * 3 // 4 if forward else place < 2**depth // 4
    return depth <= DIRECT


def far_above(low_task, high_task):
    depth, first, size = low_task
    up_depth, up_first, up_size = high_task
    if up_depth > depth - 2:
        return False
    above = {(n + 1) // 2 ** (depth - up_depth) - 1 for n in range(first, first + size)}
    return any(up_first <= p < up_first + up_size for p in above)


def make_kernel(A, B, Y, NS, R, WC, WR):
    r = R // (A * B)
    half = R // 2
    inner = 2 ** (LEV - 1) - 1

    def kernel(
        rhs_h, fac_h, inv_h, pat, sol_h, fwd_h,
        rhs, fac, inv, src, recv1, recv2, recv3, recv4, yout, tout, csrc, cr_f, cr_b, yr_f, yr_b, sol,
        lsem, ssem, rsem,
    ):
        prow = lax.axis_index("prow")
        pcol = lax.axis_index("pcol")
        my_a, my_b = prow // B, prow % B
        my_y, my_c = pcol // 2, pcol % 2
        other_c = 1 - my_c
        counter = [0]
        lcounter = [0]

        loads = {}

        def load(key, source, target):
            copy = pltpu.make_async_copy(source, target, lsem.at[lcounter[0]])
            lcounter[0] += 1
            copy.start()
            loads[key] = copy

        def need(key):
            if key in loads:
                loads.pop(key).wait()

        for depth in range(LEV - 1, -1, -1):
            count = 2**depth
            nodes = pl.ds(count - 1, count)
            load(("rhs", depth), rhs_h.at[nodes], rhs.at[nodes])
            load(("inv", depth), inv_h.at[nodes], inv.at[nodes])
            if depth:
                blocks = pl.ds(block_start(depth), count * depth)
                load(("fac", depth), fac_h.at[blocks], fac.at[blocks])

        barrier = pltpu.get_barrier_semaphore()
        peers = [{"prow": (prow + o) % (A * B)} for o in range(1, A * B)]
        peers += [{"pcol": (pcol + o) % (2 * Y)} for o in range(1, 2 * Y)]
        for peer in peers:
            pl.semaphore_signal(barrier, inc=1, device_id=peer, device_id_type=MESH)
        csrc[...] = jnp.zeros(csrc.shape, jnp.float32)
        pl.semaphore_wait(barrier, len(peers))

        def send(source, target, peer):
            k = counter[0]
            counter[0] += 1
            copy = pltpu.make_async_remote_copy(
                src_ref=source, dst_ref=target, send_sem=ssem.at[k], recv_sem=rsem.at[k],
                device_id=peer, device_id_type=MESH,
            )
            copy.start()
            return copy

        def wait_all(copies):
            for copy in copies:
                copy.wait()

        def put_parts(value, n):
            for q in range(A * B):
                src[q % B, q // B, n] = value[q * r : (q + 1) * r]

        def get_parts(ref, n):
            return jnp.concatenate(
                [ref[q % B, q // B, n] for q in range(A * B)], axis=0
            )

        def get_halves(ref, n):
            return jnp.concatenate([ref[0, n], ref[1, n]], axis=0)

        def reduce_rows_direct(first, size, out, finish):
            nodes = pl.ds(first, size)
            others = [(prow + o) % (A * B) for o in range(1, A * B)]
            copies = []
            for k, q in enumerate(others):
                copies.append(
                    send(src.at[q % B, q // B, nodes], recv3.at[k, nodes], {"prow": q})
                )
            yield
            wait_all(copies)
            total = src[my_b, my_a, nodes]
            for k in range(A * B - 1):
                total = total + recv3[k, nodes]
            out[my_b, my_a, nodes] = finish(total, nodes)
            part = out.at[my_b, my_a, nodes]
            copies = [send(part, part, {"prow": q}) for q in others]
            yield
            wait_all(copies)

        def reduce_rows(depth, first, size, out, finish):
            if few_in_flight(depth, first, out is yout):
                yield from reduce_rows_direct(first, size, out, finish)
                return
            nodes = pl.ds(first, size)
            copies = []
            for o in range(1, B):
                b = (my_b + o) % B
                copies.append(
                    send(src.at[b, :, nodes], recv1.at[o - 1, :, nodes], {"prow": my_a * B + b})
                )
            yield
            wait_all(copies)
            for o in range(1, B):
                src[my_b, :, nodes] += recv1[o - 1, :, nodes]
            copies = []
            for o in range(1, A):
                a = (my_a + o) % A
                copies.append(
                    send(src.at[my_b, a, nodes], recv2.at[o - 1, nodes], {"prow": a * B + my_b})
                )
            yield
            wait_all(copies)
            total = src[my_b, my_a, nodes]
            for o in range(1, A):
                total = total + recv2[o - 1, nodes]
            out[my_b, my_a, nodes] = finish(total, nodes)
            copies = []
            for o in range(1, A):
                a = (my_a + o) % A
                part = out.at[my_b, my_a, nodes]
                copies.append(send(part, part, {"prow": a * B + my_b}))
            yield
            wait_all(copies)
            copies = []
            for o in range(1, B):
                b = (my_b + o) % B
                part = out.at[my_b, :, nodes]
                copies.append(send(part, part, {"prow": my_a * B + b}))
            yield
            wait_all(copies)

        def reduce_columns_direct(first, size, slot, finish):
            nodes, slots = pl.ds(first, size), pl.ds(slot, size)
            recv4[pcol, slots] = jnp.stack([csrc[0, nodes], csrc[1, nodes]], axis=1)
            copies = []
            for o in range(1, 2 * Y):
                part = recv4.at[pcol, slots]
                copies.append(send(part, part, {"pcol": (pcol + o) % (2 * Y)}))
            yield
            wait_all(copies)
            for c in range(2):
                total = recv4[0, slots, c]
                for q in range(1, 2 * Y):
                    total = total + recv4[q, slots, c]
                sol[c, nodes] = finish(total, nodes, pl.ds(c * half, half))

        def reduce_columns(depth, first, size, cr, yr, out, finish):
            if depth <= DIRECT:
                slot = 2 ** (DIRECT + 1) - 1 if cr is cr_b and depth == 0 else first
                yield from reduce_columns_direct(first, size, slot, finish)
                return
            mine = pl.ds(pl.multiple_of(my_c * half, half), half)
            nodes = pl.ds(first, size)
            core = {"pcol": my_y * 2 + other_c}
            copies = [send(csrc.at[other_c, nodes], cr.at[nodes], core)]
            yield
            wait_all(copies)
            yr[my_y, nodes] = csrc[my_c, nodes] + cr[nodes]
            copies = []
            for o in range(1, Y):
                part = yr.at[my_y, nodes]
                copies.append(send(part, part, {"pcol": ((my_y + o) % Y) * 2 + my_c}))
            yield
            wait_all(copies)
            total = yr[0, nodes]
            for y in range(1, Y):
                total = total + yr[y, nodes]
            out[my_c, nodes] = finish(total, nodes, mine)
            part = out.at[my_c, nodes]
            copies = [send(part, part, core)]
            yield
            wait_all(copies)

        def forward_task(depth, first, size):
            need(("rhs", depth))
            if depth < LEV - 1:
                yield from reduce_columns(
                    depth, first, size, cr_f, yr_f, sol,
                    lambda total, nodes, mine: rhs[nodes, mine] - total,
                )
                yield "matmul"
            need(("inv", depth))

            def solve(n, _):
                value = rhs[n] if depth == LEV - 1 else get_halves(sol, n)
                put_parts(
                    lax.dot_general(
                        value.astype(jnp.bfloat16), inv[n], (((1,), (1,)), ((), ())),
                        preferred_element_type=jnp.float32,
                    ),
                    n,
                )
                return _

            lax.fori_loop(first, first + size, solve, 0, unroll=True)
            yield from reduce_rows(depth, first, size, yout, lambda total, nodes: total)
            if depth:
                yield "matmul"
                push_up(depth, first, size, [1])

        def push_up(depth, first, size, ups):
            need(("fac", depth))
            start = block_start(depth)

            def push(m, _):
                narrow = get_parts(yout, m)
                base = start + (m - (2**depth - 1)) * depth
                for up in ups:
                    weight = pat[base + up - 1].astype(jnp.float32)
                    terms = lax.dot_general(
                        narrow.astype(jnp.bfloat16), fac[base + up - 1],
                        (((1,), (1,)), ((), ())), preferred_element_type=jnp.float32,
                    ) * weight
                    above = (m + 1) // 2**up - 1
                    csrc[0, above] += terms[:half]
                    csrc[1, above] += terms[half:]
                return _

            lax.fori_loop(first, first + size, push, 0, unroll=True)

        def pull_down(depth, first, size, ups, add):
            start = block_start(depth)

            def pull(n, _):
                base = start + (n - (2**depth - 1)) * depth
                total = get_parts(src, n) if add else jnp.zeros((R, WC), jnp.float32)
                for up in ups:
                    above = (n + 1) // 2**up - 1
                    weight = pat[base + up - 1].astype(jnp.float32)
                    total = total + weight * jnp.dot(
                        get_halves(sol, above).astype(jnp.bfloat16), fac[base + up - 1],
                        preferred_element_type=jnp.float32,
                    )
                put_parts(total, n)
                return _

            lax.fori_loop(first, first + size, pull, 0, unroll=True)

        def backward_task(depth, first, size):
            if depth:
                pull_down(depth, first, size, [1], depth > 1)
                yield from reduce_rows(
                    depth, first, size, tout,
                    lambda total, nodes: yout[my_b, my_a, nodes] - total,
                )
                yield "matmul"
            target = tout if depth else yout

            def solve(n, _):
                value = jnp.dot(
                    get_parts(target, n).astype(jnp.bfloat16), inv[n],
                    preferred_element_type=jnp.float32,
                )
                csrc[0, n] = value[:half]
                csrc[1, n] = value[half:]
                return _

            lax.fori_loop(first, first + size, solve, 0, unroll=True)
            yield from reduce_columns(
                depth, first, size, cr_b, yr_b, sol, lambda total, nodes, mine: total
            )

        up_tasks = tasks_of(range(LEV - 1, -1, -1))
        late = {
            t: functools.partial(push_up, *t, range(2, t[0] + 1)) for t in up_tasks if t[0] > 1
        }
        run_tasks(
            up_tasks, forward_task, lambda task, other: overlaps(other, task),
            late, lambda filler, other: other == filler, far_above,
        )
        out_copy = pltpu.make_async_copy(yout, fwd_h, lsem.at[lcounter[0]])
        out_copy.start()
        down_tasks = tasks_of(range(LEV))
        early = {
            t: functools.partial(pull_down, *t, range(2, t[0] + 1), False)
            for t in down_tasks if t[0] > 1
        }
        run_tasks(
            down_tasks, backward_task, overlaps,
            early, far_above, lambda filler, task: filler == task,
        )
        sol_copy = pltpu.make_async_copy(sol, sol_h, lsem.at[lcounter[0] + 1])
        sol_copy.start()
        out_copy.wait()
        sol_copy.wait()

    f32, bf16 = jnp.float32, jnp.bfloat16
    sends = 0
    for depth in range(LEV):
        rows = A * B - 1 if depth <= DIRECT + 1 else A + B - 2
        cols = 2 * Y - 1 if depth <= DIRECT else 1 + Y
        sends += CHUNKS[depth] * 2 * (2 * rows + cols)
    blocks = block_start(LEV)
    scratch = [
        pltpu.VMEM((NS, R, WR), f32),
        pltpu.VMEM((blocks, WR, WC), bf16),
        pltpu.VMEM((NS, WC, WR), bf16),
        pltpu.VMEM((B, A, NS, r, WC), f32),
        pltpu.VMEM((B - 1, A, NS, r, WC), f32),
        pltpu.VMEM((A - 1, NS, r, WC), f32),
        pltpu.VMEM((A * B - 1, 2 ** (DIRECT + 2) - 1, r, WC), f32),
        pltpu.VMEM((2 * Y, 2 ** (DIRECT + 1), 2, half, WR), f32),
        pltpu.VMEM((B, A, NS, r, WC), f32),
        pltpu.VMEM((B, A, NS, r, WC), f32),
        pltpu.VMEM((2, NS, half, WR), f32),
        pltpu.VMEM((inner, half, WR), f32),
        pltpu.VMEM((NS, half, WR), f32),
        pltpu.VMEM((Y, inner, half, WR), f32),
        pltpu.VMEM((Y, NS, half, WR), f32),
        pltpu.VMEM((2, NS, half, WR), f32),
        pltpu.SemaphoreType.DMA((3 * LEV + 2,)),
        pltpu.SemaphoreType.DMA((sends,)),
        pltpu.SemaphoreType.DMA((sends,)),
    ]
    any_spec = pl.BlockSpec(memory_space=pl.ANY)
    return pl.pallas_call(
        kernel,
        out_shape=(
            jax.ShapeDtypeStruct((2, NS, half, WR), f32),
            jax.ShapeDtypeStruct((B, A, NS, r, WC), f32),
        ),
        in_specs=[any_spec, any_spec, any_spec, pl.BlockSpec(memory_space=pltpu.SMEM)],
        out_specs=(any_spec, any_spec),
        scratch_shapes=scratch,
        cost_estimate=pl.CostEstimate(
            flops=4 * R * WR * WC * (blocks + NS),
            bytes_accessed=2 * WR * WC * (blocks + NS) + 8 * NS * R * (WC + WR),
            transcendentals=0,
        ),
        compiler_params=pltpu.CompilerParams(
            collective_id=0, has_side_effects=True, vmem_limit_bytes=64 * 1024 * 1024 - 65536
        ),
    )


def solution(mesh):
    A, B = split_rows(mesh.shape["prow"])
    Y = mesh.shape["pcol"] // 2

    def per_device(rhs, factor, inverse, pattern):
        NS, R, WR = rhs.shape
        WC = inverse.shape[1]
        sol, fwd = make_kernel(A, B, Y, NS, R, WC, WR)(rhs, factor, inverse, pattern)
        sol = jnp.transpose(sol, (1, 0, 2, 3)).reshape(NS, R, WR)
        fwd = jnp.transpose(fwd, (2, 1, 0, 3, 4)).reshape(NS, R, WC)
        return sol, fwd

    in_specs = (P(None, None, "prow"), P(None, "prow", "pcol"), P(None, "pcol", "prow"), P())
    out_specs = (P(None, None, "prow"), P(None, None, "pcol"))
    return jax.shard_map(
        per_device, mesh=mesh, in_specs=in_specs, out_specs=out_specs, check_vma=False
    )
```

```python
import functools

import jax
import jax.numpy as jnp
from jax import lax
from jax.experimental import pallas as pl
from jax.experimental.pallas import tpu as pltpu
from jax.sharding import PartitionSpec as P

LEV = 5
CHUNKS = {4: 4, 3: 4, 2: 2, 1: 1, 0: 1}
DIRECT = 2
MESH = pl.DeviceIdType.MESH


def block_start(tree_depth):
    return (tree_depth - 2) * 2**tree_depth + 2


def split_rows(prow):
    minor = 1
    while minor * minor * 4 <= prow:
        minor *= 2
    return prow // minor, minor


def tasks_of(order):
    tasks = []
    for depth in order:
        size = 2**depth // CHUNKS[depth]
        for c in range(CHUNKS[depth]):
            tasks.append((depth, 2**depth - 1 + c * size, size))
    return tasks


def run_tasks(tasks, make, needs, fillers, filler_needs, blocks):
    done = set()
    live = {}
    heavy = []
    waiting = list(tasks)
    left = list(fillers)

    def advance(task):
        try:
            if next(live[task]) == "matmul":
                heavy.append(task)
        except StopIteration:
            done.add(task)
            del live[task]

    while waiting or live or left:
        started = set()
        for task in list(waiting):
            ready = all(other in done for other in tasks if needs(task, other))
            ready = ready and not any(blocks(filler, task) for filler in left)
            if ready and task[0] not in started:
                started.add(task[0])
                live[task] = make(*task)
                waiting.remove(task)
        for task in list(live):
            if task not in heavy:
                advance(task)
        for task in list(heavy):
            heavy.remove(task)
            advance(task)
        for filler in list(left):
            if all(other in done for other in tasks if filler_needs(filler, other)):
                left.remove(filler)
                fillers[filler]()
                break


def overlaps(low_task, high_task):
    depth, first, size = low_task
    up_depth, up_first, up_size = high_task
    if up_depth != depth - 1:
        return False
    parents = {(n + 1) // 2 - 1 for n in range(first, first + size)}
    return any(up_first <= p < up_first + up_size for p in parents)


def few_in_flight(depth, first, forward):
    if depth == DIRECT + 1:
        place = first - (2**depth - 1)
        return place >= 2**depth * 3 // 4 if forward else place < 2**depth // 4
    return depth <= DIRECT


def far_above(low_task, high_task):
    depth, first, size = low_task
    up_depth, up_first, up_size = high_task
    if up_depth > depth - 2:
        return False
    above = {(n + 1) // 2 ** (depth - up_depth) - 1 for n in range(first, first + size)}
    return any(up_first <= p < up_first + up_size for p in above)


def make_kernel(A, B, Y, NS, R, WC, WR):
    r = R // (A * B)
    half = R // 2
    inner = 2 ** (LEV - 1) - 1

    def kernel(
        rhs_h, fac_h, inv_h, pat, sol_h, fwd_h,
        rhs, fac, inv, src, recv1, recv2, recv3, recv4, yout, tout, csrc, cr_f, cr_b, yr_f, yr_b, sol,
        lsem, ssem, rsem,
    ):
        prow = lax.axis_index("prow")
        pcol = lax.axis_index("pcol")
        my_a, my_b = prow // B, prow % B
        my_y, my_c = pcol // 2, pcol % 2
        other_c = 1 - my_c
        counter = [0]
        lcounter = [0]

        loads = {}

        def load(key, source, target):
            copy = pltpu.make_async_copy(source, target, lsem.at[lcounter[0]])
            lcounter[0] += 1
            copy.start()
            loads[key] = copy

        def need(key):
            if key in loads:
                loads.pop(key).wait()

        for depth in range(LEV - 1, -1, -1):
            count = 2**depth
            nodes = pl.ds(count - 1, count)
            load(("rhs", depth), rhs_h.at[nodes], rhs.at[nodes])
            load(("inv", depth), inv_h.at[nodes], inv.at[nodes])
            if depth:
                blocks = pl.ds(block_start(depth), count * depth)
                load(("fac", depth), fac_h.at[blocks], fac.at[blocks])

        barrier = pltpu.get_barrier_semaphore()
        peers = [{"prow": (prow + o) % (A * B)} for o in range(1, A * B)]
        peers += [{"pcol": (pcol + o) % (2 * Y)} for o in range(1, 2 * Y)]
        for peer in peers:
            pl.semaphore_signal(barrier, inc=1, device_id=peer, device_id_type=MESH)
        csrc[...] = jnp.zeros(csrc.shape, jnp.float32)
        pl.semaphore_wait(barrier, len(peers))

        def send(source, target, peer):
            k = counter[0]
            counter[0] += 1
            copy = pltpu.make_async_remote_copy(
                src_ref=source, dst_ref=target, send_sem=ssem.at[k], recv_sem=rsem.at[k],
                device_id=peer, device_id_type=MESH,
            )
            copy.start()
            return copy

        def wait_all(copies):
            for copy in copies:
                copy.wait()

        def put_parts(value, n):
            for q in range(A * B):
                src[q % B, q // B, n] = value[q * r : (q + 1) * r]

        def get_parts(ref, n):
            return jnp.concatenate(
                [ref[q % B, q // B, n] for q in range(A * B)], axis=0
            )

        def get_halves(ref, n):
            return jnp.concatenate([ref[0, n], ref[1, n]], axis=0)

        def reduce_rows_direct(first, size, out, finish):
            nodes = pl.ds(first, size)
            others = [(prow + o) % (A * B) for o in range(1, A * B)]
            copies = []
            for k, q in enumerate(others):
                copies.append(
                    send(src.at[q % B, q // B, nodes], recv3.at[k, nodes], {"prow": q})
                )
            yield
            wait_all(copies)
            total = src[my_b, my_a, nodes]
            for k in range(A * B - 1):
                total = total + recv3[k, nodes]
            out[my_b, my_a, nodes] = finish(total, nodes)
            part = out.at[my_b, my_a, nodes]
            copies = [send(part, part, {"prow": q}) for q in others]
            yield
            wait_all(copies)

        def reduce_rows(depth, first, size, out, finish):
            if few_in_flight(depth, first, out is yout):
                yield from reduce_rows_direct(first, size, out, finish)
                return
            nodes = pl.ds(first, size)
            copies = []
            for o in range(1, B):
                b = (my_b + o) % B
                copies.append(
                    send(src.at[b, :, nodes], recv1.at[o - 1, :, nodes], {"prow": my_a * B + b})
                )
            yield
            wait_all(copies)
            for o in range(1, B):
                src[my_b, :, nodes] += recv1[o - 1, :, nodes]
            copies = []
            for o in range(1, A):
                a = (my_a + o) % A
                copies.append(
                    send(src.at[my_b, a, nodes], recv2.at[o - 1, nodes], {"prow": a * B + my_b})
                )
            yield
            wait_all(copies)
            total = src[my_b, my_a, nodes]
            for o in range(1, A):
                total = total + recv2[o - 1, nodes]
            out[my_b, my_a, nodes] = finish(total, nodes)
            copies = []
            for o in range(1, A):
                a = (my_a + o) % A
                part = out.at[my_b, my_a, nodes]
                copies.append(send(part, part, {"prow": a * B + my_b}))
            yield
            wait_all(copies)
            copies = []
            for o in range(1, B):
                b = (my_b + o) % B
                part = out.at[my_b, :, nodes]
                copies.append(send(part, part, {"prow": my_a * B + b}))
            yield
            wait_all(copies)

        def reduce_columns_direct(first, size, slot, finish):
            nodes, slots = pl.ds(first, size), pl.ds(slot, size)
            recv4[pcol, slots] = jnp.stack([csrc[0, nodes], csrc[1, nodes]], axis=1)
            copies = []
            for o in range(1, 2 * Y):
                part = recv4.at[pcol, slots]
                copies.append(send(part, part, {"pcol": (pcol + o) % (2 * Y)}))
            yield
            wait_all(copies)
            for c in range(2):
                total = recv4[0, slots, c]
                for q in range(1, 2 * Y):
                    total = total + recv4[q, slots, c]
                sol[c, nodes] = finish(total, nodes, pl.ds(c * half, half))

        def reduce_columns(depth, first, size, cr, yr, out, finish):
            if depth <= DIRECT:
                slot = 2 ** (DIRECT + 1) - 1 if cr is cr_b and depth == 0 else first
                yield from reduce_columns_direct(first, size, slot, finish)
                return
            mine = pl.ds(pl.multiple_of(my_c * half, half), half)
            nodes = pl.ds(first, size)
            core = {"pcol": my_y * 2 + other_c}
            copies = [send(csrc.at[other_c, nodes], cr.at[nodes], core)]
            yield
            wait_all(copies)
            yr[my_y, nodes] = csrc[my_c, nodes] + cr[nodes]
            copies = []
            for o in range(1, Y):
                part = yr.at[my_y, nodes]
                copies.append(send(part, part, {"pcol": ((my_y + o) % Y) * 2 + my_c}))
            yield
            wait_all(copies)
            total = yr[0, nodes]
            for y in range(1, Y):
                total = total + yr[y, nodes]
            out[my_c, nodes] = finish(total, nodes, mine)
            part = out.at[my_c, nodes]
            copies = [send(part, part, core)]
            yield
            wait_all(copies)

        def forward_task(depth, first, size):
            need(("rhs", depth))
            if depth < LEV - 1:
                yield from reduce_columns(
                    depth, first, size, cr_f, yr_f, sol,
                    lambda total, nodes, mine: rhs[nodes, mine] - total,
                )
                yield "matmul"
            need(("inv", depth))

            def solve(n, _):
                value = rhs[n] if depth == LEV - 1 else get_halves(sol, n)
                put_parts(
                    lax.dot_general(
                        value.astype(jnp.bfloat16), inv[n], (((1,), (1,)), ((), ())),
                        preferred_element_type=jnp.float32,
                    ),
                    n,
                )
                return _

            lax.fori_loop(first, first + size, solve, 0)
            yield from reduce_rows(depth, first, size, yout, lambda total, nodes: total)
            if depth:
                yield "matmul"
                push_up(depth, first, size, [1])

        def push_up(depth, first, size, ups):
            need(("fac", depth))
            start = block_start(depth)

            def push(m, _):
                narrow = get_parts(yout, m)
                base = start + (m - (2**depth - 1)) * depth
                for up in ups:
                    weight = pat[base + up - 1].astype(jnp.float32)
                    terms = lax.dot_general(
                        narrow.astype(jnp.bfloat16), fac[base + up - 1],
                        (((1,), (1,)), ((), ())), preferred_element_type=jnp.float32,
                    ) * weight
                    above = (m + 1) // 2**up - 1
                    csrc[0, above] += terms[:half]
                    csrc[1, above] += terms[half:]
                return _

            lax.fori_loop(first, first + size, push, 0)

        def pull_down(depth, first, size, ups, add):
            start = block_start(depth)

            def pull(n, _):
                base = start + (n - (2**depth - 1)) * depth
                total = get_parts(src, n) if add else jnp.zeros((R, WC), jnp.float32)
                for up in ups:
                    above = (n + 1) // 2**up - 1
                    weight = pat[base + up - 1].astype(jnp.float32)
                    total = total + weight * jnp.dot(
                        get_halves(sol, above).astype(jnp.bfloat16), fac[base + up - 1],
                        preferred_element_type=jnp.float32,
                    )
                put_parts(total, n)
                return _

            lax.fori_loop(first, first + size, pull, 0)

        def backward_task(depth, first, size):
            if depth:
                pull_down(depth, first, size, [1], depth > 1)
                yield from reduce_rows(
                    depth, first, size, tout,
                    lambda total, nodes: yout[my_b, my_a, nodes] - total,
                )
                yield "matmul"
            target = tout if depth else yout

            def solve(n, _):
                value = jnp.dot(
                    get_parts(target, n).astype(jnp.bfloat16), inv[n],
                    preferred_element_type=jnp.float32,
                )
                csrc[0, n] = value[:half]
                csrc[1, n] = value[half:]
                return _

            lax.fori_loop(first, first + size, solve, 0)
            yield from reduce_columns(
                depth, first, size, cr_b, yr_b, sol, lambda total, nodes, mine: total
            )

        up_tasks = tasks_of(range(LEV - 1, -1, -1))
        late = {
            t: functools.partial(push_up, *t, range(2, t[0] + 1)) for t in up_tasks if t[0] > 1
        }
        run_tasks(
            up_tasks, forward_task, lambda task, other: overlaps(other, task),
            late, lambda filler, other: other == filler, far_above,
        )
        out_copy = pltpu.make_async_copy(yout, fwd_h, lsem.at[lcounter[0]])
        out_copy.start()
        down_tasks = tasks_of(range(LEV))
        early = {
            t: functools.partial(pull_down, *t, range(2, t[0] + 1), False)
            for t in down_tasks if t[0] > 1
        }
        run_tasks(
            down_tasks, backward_task, overlaps,
            early, far_above, lambda filler, task: filler == task,
        )
        sol_copy = pltpu.make_async_copy(sol, sol_h, lsem.at[lcounter[0] + 1])
        sol_copy.start()
        out_copy.wait()
        sol_copy.wait()

    f32, bf16 = jnp.float32, jnp.bfloat16
    sends = 0
    for depth in range(LEV):
        rows = A * B - 1 if depth <= DIRECT + 1 else A + B - 2
        cols = 2 * Y - 1 if depth <= DIRECT else 1 + Y
        sends += CHUNKS[depth] * 2 * (2 * rows + cols)
    blocks = block_start(LEV)
    scratch = [
        pltpu.VMEM((NS, R, WR), f32),
        pltpu.VMEM((blocks, WR, WC), bf16),
        pltpu.VMEM((NS, WC, WR), bf16),
        pltpu.VMEM((B, A, NS, r, WC), f32),
        pltpu.VMEM((B - 1, A, NS, r, WC), f32),
        pltpu.VMEM((A - 1, NS, r, WC), f32),
        pltpu.VMEM((A * B - 1, 2 ** (DIRECT + 2) - 1, r, WC), f32),
        pltpu.VMEM((2 * Y, 2 ** (DIRECT + 1), 2, half, WR), f32),
        pltpu.VMEM((B, A, NS, r, WC), f32),
        pltpu.VMEM((B, A, NS, r, WC), f32),
        pltpu.VMEM((2, NS, half, WR), f32),
        pltpu.VMEM((inner, half, WR), f32),
        pltpu.VMEM((NS, half, WR), f32),
        pltpu.VMEM((Y, inner, half, WR), f32),
        pltpu.VMEM((Y, NS, half, WR), f32),
        pltpu.VMEM((2, NS, half, WR), f32),
        pltpu.SemaphoreType.DMA((3 * LEV + 2,)),
        pltpu.SemaphoreType.DMA((sends,)),
        pltpu.SemaphoreType.DMA((sends,)),
    ]
    any_spec = pl.BlockSpec(memory_space=pl.ANY)
    return pl.pallas_call(
        kernel,
        out_shape=(
            jax.ShapeDtypeStruct((2, NS, half, WR), f32),
            jax.ShapeDtypeStruct((B, A, NS, r, WC), f32),
        ),
        in_specs=[any_spec, any_spec, any_spec, pl.BlockSpec(memory_space=pltpu.SMEM)],
        out_specs=(any_spec, any_spec),
        scratch_shapes=scratch,
        cost_estimate=pl.CostEstimate(
            flops=4 * R * WR * WC * (blocks + NS),
            bytes_accessed=2 * WR * WC * (blocks + NS) + 8 * NS * R * (WC + WR),
            transcendentals=0,
        ),
        compiler_params=pltpu.CompilerParams(
            collective_id=0, has_side_effects=True, vmem_limit_bytes=64 * 1024 * 1024 - 65536
        ),
    )


def solution(mesh):
    A, B = split_rows(mesh.shape["prow"])
    Y = mesh.shape["pcol"] // 2

    def per_device(rhs, factor, inverse, pattern):
        NS, R, WR = rhs.shape
        WC = inverse.shape[1]
        sol, fwd = make_kernel(A, B, Y, NS, R, WC, WR)(rhs, factor, inverse, pattern)
        sol = jnp.transpose(sol, (1, 0, 2, 3)).reshape(NS, R, WR)
        fwd = jnp.transpose(fwd, (2, 1, 0, 3, 4)).reshape(NS, R, WC)
        return sol, fwd

    in_specs = (P(None, None, "prow"), P(None, "prow", "pcol"), P(None, "pcol", "prow"), P())
    out_specs = (P(None, None, "prow"), P(None, None, "pcol"))
    return jax.shard_map(
        per_device, mesh=mesh, in_specs=in_specs, out_specs=out_specs, check_vma=False
    )
```
